32 devices in a mesh: grp: 2 (over x), lon: 16 (over z, y, core).
Axes of the slice: x: 2, y: 2, z: 4, core: 2. Of those that a mesh axis runs over, the one named last changes fastest.
Arguments:
- tracers: float32 [10, 4, 256, 2880], P('grp', None, 'lon'), parts along dimension 0, may hold values from -6 to 6
- east_courant: float32 [8, 256, 2880], P('grp', 'lon'), parts along dimension 0, may hold values from -0.3 to 0.3
- north_courant: float32 [8, 256, 2880], P('grp', 'lon'), parts along dimension 0, may hold values from -0.3 to 0.3
- spectrum: float32 [64, 2880], replicated, may hold values from 0.05 to 1
- filter_index: int32 [256], replicated, may hold values from 0 to 63
Outputs:
- updated: float32 [10, 4, 256, 2880], P('grp', None, 'lon'), parts along dimension 0
The draws below stay inside these ranges and needn't reach their ends.
There are 2 independent parts, one for each index of `grp`. The reference program is written for one: setup_inputs(seed, part) draws one part's arguments, and reference() takes and returns one part's arrays. A program takes and returns all parts, laid end to end along the dimension named above; an argument that names none is the same for every part. Nothing has to cross between parts.
All inputs are finite; a program needn't handle non-finite values.
Results may differ from the reference program's by a relative error of at most 0.00075.
Values may be sent and summed in bfloat16 or wider, within the bound.
A program may use at most 128 MiB of HBM per device.

```python
import math
import jax
import jax.numpy as jnp
from jax import lax

FIELDS = 5
LEVELS = 4
NLON = 2880
FILTERS = 64
NLAT = 256


def plant(entries, rng, smallest, high):
    longest = entries.shape.index(max(entries.shape))
    spots = []
    for shift in (0, 1):
        where = [jax.random.randint(jax.random.fold_in(rng, axis), (), 0, length) for axis, length in enumerate(entries.shape)]
        where[longest] = (where[longest] + shift) % entries.shape[longest]
        spots.append(tuple(where))
    return entries.at[spots[0]].set(smallest).at[spots[1]].set(high)


def steps_of(own_key, shape, shards, least, largest):
    def one(axis_at, parts):
        draws = jax.random.uniform(jax.random.fold_in(jax.random.fold_in(own_key, 6), axis_at), (parts,), jnp.float32, least / len(shards), largest / len(shards))
        return jnp.repeat(jnp.exp(draws), shape[axis_at] // parts).reshape((-1,) + (1,) * (len(shape) - axis_at - 1))

    gain = one(*shards[0])
    for cut in shards[1:]:
        gain = gain * one(*cut)
    return gain


def gaussian(own_key, extent, deviation, reach, split=(), kind=jnp.bfloat16):
    array = jax.random.normal(own_key, extent, jnp.float32) * deviation
    if len(split) > 0:
        array = steps_of(own_key, extent, split, -0.22, 0.18) * array
    return jnp.clip(array, min=-reach, max=reach).astype(kind)


def setup_inputs(seed: int = 0, part: int = 0) -> dict:
    splits = jax.random.split(jax.random.key(seed), 6)
    part_keys = jax.random.split(jax.random.fold_in(splits[5], part), 6)
    tracers = gaussian(part_keys[0], (FIELDS, LEVELS, NLAT, NLON), 1.0, 6.0, ((2, 16),), jnp.float32)
    east_courant = jnp.clip(jax.random.uniform(part_keys[1], (LEVELS, NLAT, NLON), jnp.float32, -0.3, 0.3) * steps_of(part_keys[1], (LEVELS, NLAT, NLON), ((1, 16),), -0.4, 0.0), -0.3, 0.3)
    north_courant = jnp.clip(jax.random.uniform(part_keys[2], (LEVELS, NLAT, NLON), jnp.float32, -0.3, 0.3) * steps_of(part_keys[2], (LEVELS, NLAT, NLON), ((1, 16),), -0.4, 0.0), -0.3, 0.3)
    spectrum = jnp.clip(jnp.exp(jax.random.uniform(splits[3], (FILTERS, NLON), jnp.float32, math.log(0.05), math.log(1.0))), 0.05, 1.0)
    filter_index = plant(jax.random.randint(splits[4], (NLAT,), 0, FILTERS), jax.random.fold_in(splits[4], 1), 0, FILTERS - 1).astype(jnp.int32)
    return dict(tracers=tracers, east_courant=east_courant, north_courant=north_courant, spectrum=spectrum, filter_index=filter_index)


def min_mod(left, right):
    return jnp.maximum(jnp.minimum(left, right), 0.0) + jnp.minimum(jnp.maximum(left, right), 0.0)


def face_flux(left_q, left_s, right_q, right_s, courant):
    return jnp.maximum(courant, 0.0) * (left_q + 0.5 * (1.0 - courant) * left_s) + jnp.minimum(courant, 0.0) * (right_q - 0.5 * (1.0 + courant) * right_s)


def tendency(padded, south_courant, north_courant, east_courant, global_rows, total_rows):
    center = padded[:, :, 2:-2]
    slopes = min_mod(padded[:, :, 2:] - padded[:, :, 1:-1], padded[:, :, 1:-1] - padded[:, :, :-2])
    north = face_flux(center, slopes[:, :, 1:-1], padded[:, :, 3:-1], slopes[:, :, 2:], north_courant[None])
    south = face_flux(padded[:, :, 1:-3], slopes[:, :, :-2], center, slopes[:, :, 1:-1], south_courant[None])
    eastern = jnp.roll(center, -1, axis=3)
    western = jnp.roll(center, 1, axis=3)
    slope_x = min_mod(eastern - center, center - western)
    east = face_flux(center, slope_x, eastern, jnp.roll(slope_x, -1, axis=3), east_courant[None])
    west = jnp.roll(east, 1, axis=3)
    spacing = math.pi / total_rows
    row_float = global_rows.astype(jnp.float32)
    cos_north = jnp.sin((row_float + 1.0) * spacing)[:, None]
    cos_south = jnp.sin(row_float * spacing)[:, None]
    cos_center = jnp.sin((row_float + 0.5) * spacing)[:, None]
    return -(east - west) - (cos_north * north - cos_south * south) / cos_center


def make_basis(width):
    half_width = width // 2
    points = jnp.arange(width, dtype=jnp.int32)[:, None]
    column = jnp.arange(width, dtype=jnp.int32)[None, :]
    number = jnp.where(column <= half_width, column, column - half_width)
    phase = (points * number) % width
    angle = phase.astype(jnp.float32) * (2.0 * math.pi / width)
    basis = jnp.where(column <= half_width, jnp.cos(angle), jnp.sin(angle)).astype(jnp.bfloat16)
    flat_col = jnp.arange(width, dtype=jnp.int32)
    weights = jnp.where((flat_col == 0) | (flat_col == half_width), 1.0 / width, 2.0 / width).astype(jnp.float32)
    return basis, weights


def filter_block(band, index_rows, basis, weights, spectrum):
    fields, levels, count, width = band.shape
    one_hot = (index_rows[:, None] == jnp.arange(spectrum.shape[0], dtype=jnp.int32)[None, :]).astype(jnp.float32)
    response = jnp.dot(one_hot, spectrum, precision=lax.Precision.HIGHEST, preferred_element_type=jnp.float32) * weights[None, :]
    flat = band.reshape(fields * levels * count, width)
    coefficients = jnp.dot(flat, basis, preferred_element_type=jnp.float32).reshape(fields, levels, count, width)
    scaled = (coefficients * response[None, None]).astype(jnp.bfloat16).reshape(fields * levels * count, width)
    result = lax.dot_general(scaled, basis, (((1,), (1,)), ((), ())), preferred_element_type=jnp.float32)
    return result.reshape(fields, levels, count, width)


def reference(tracers, east_courant, north_courant, spectrum, filter_index):
    padded = jnp.pad(tracers, ((0, 0), (0, 0), (2, 2), (0, 0)))
    zero_row = jnp.zeros((LEVELS, 1, NLON), jnp.float32)
    south_courant = jnp.concatenate([zero_row, north_courant[:, :-1]], axis=1)
    global_rows = jnp.arange(NLAT, dtype=jnp.int32)
    increment = tendency(padded, south_courant, north_courant, east_courant, global_rows, NLAT)
    basis, weights = make_basis(NLON)
    quarter = NLAT // 4
    south_band = filter_block(increment[:, :, :quarter].astype(jnp.bfloat16), filter_index[:quarter], basis, weights, spectrum)
    north_band = filter_block(increment[:, :, NLAT - quarter:].astype(jnp.bfloat16), filter_index[NLAT - quarter:], basis, weights, spectrum)
    change = jnp.concatenate([south_band, increment[:, :, quarter:NLAT - quarter], north_band], axis=2)
    return tracers + change
```

```python
import functools
import math

import jax
import jax.numpy as jnp
import ml_dtypes
import numpy as np
from jax import lax
from jax.experimental import pallas as pl
from jax.experimental.pallas import tpu as pltpu
from jax.sharding import PartitionSpec as P

LANES = 128
CHUNK = 256


def up_to(value, multiple):
    return -(-value // multiple) * multiple


def column_groups(width):
    half = width // 2
    column = np.arange(width)
    number = np.where(column <= half, column, column - half)
    return number, [np.where(number % 4 == 0)[0], np.where(number % 4 == 2)[0], np.where(number % 2 == 1)[0]]


def make_matrices(width):
    half, part = width // 2, width // 4
    deep = up_to(part, CHUNK)
    number, groups = column_groups(width)
    points = np.arange(half, dtype=np.int64)[:, None]
    angle = ((points * number[None, :]) % width) * (2.0 * math.pi / width)
    basis = np.where(np.arange(width)[None, :] <= half, np.cos(angle), np.sin(angle))
    even = np.zeros((2, deep, deep), np.float64)
    for at in range(2):
        even[at, :part, : len(groups[at])] = basis[:part, groups[at]]
    odd = np.zeros((2, deep, 2 * deep), np.float64)
    odd[0, :part, : len(groups[2])] = basis[:part, groups[2]]
    odd[1, :part, : len(groups[2])] = basis[part:, groups[2]]
    odd = odd.reshape(2 * deep, 2 * deep)
    kind = ml_dtypes.bfloat16
    return (
        even.astype(kind),
        odd.astype(kind),
        np.ascontiguousarray(even.transpose(0, 2, 1)).astype(kind),
        np.ascontiguousarray(odd.T).astype(kind),
    )


def min_mod(a, b):
    return jnp.maximum(jnp.minimum(a, jnp.maximum(b, 0.0)), jnp.minimum(b, 0.0))


def upwind(c, ch, ql, sl, qr, sr):
    ahead = c > 0.0
    return c * jnp.where(ahead, ql, qr) + ch * jnp.where(ahead, sl, sr)


def second(c):
    return c * (jnp.where(c > 0.0, 0.5, -0.5) - 0.5 * c)


def kernel(width, polar_ref, q_ref, ce_ref, cn_ref, cs_ref, halo_ref, ratio_ref, resp_ref,
           even_hbm, odd_hbm, even_t_hbm, odd_t_hbm, out_ref,
           che_s, chn_s, inc_s, y_s, s_s, even_s, odd_s, even_t_s, odd_t_s, sems):
    planes, rows, _ = q_ref.shape
    levels = ce_ref.shape[0]
    part = width // 4
    deep = up_to(part, CHUNK)
    full = width // LANES
    rest = width - full * LANES
    tiles = full + (1 if rest else 0)
    lane = lax.broadcasted_iota(jnp.int32, (rows, LANES), 1)
    row = lax.broadcasted_iota(jnp.int32, (rows, LANES), 0)
    copies = [
        pltpu.make_async_copy(source, target, sems.at[at])
        for at, (source, target) in enumerate(
            ((even_hbm, even_s), (odd_hbm, odd_s), (even_t_hbm, even_t_s), (odd_t_hbm, odd_t_s))
        )
    ]
    polar = polar_ref[0] == 1

    @pl.when(polar)
    def _():
        for copy in copies:
            copy.start()

    def tile_of(ref, at, t):
        if t < full:
            return ref[at, :, LANES * t : LANES * (t + 1)]
        return jnp.concatenate(
            [ref[at, :, LANES * full : width], ref[at, :, : LANES - rest]], axis=1
        )

    def prepare(level, carry):
        for t in range(tiles):
            che_s[level, :, LANES * t : LANES * (t + 1)] = second(tile_of(ce_ref, level, t))
            chn_s[level, :, LANES * t : LANES * (t + 1)] = second(tile_of(cn_ref, level, t))
        return carry

    lax.fori_loop(0, levels, prepare, 0)

    def increments(p, level, put):
        memo = {}

        def cached(function):
            def call(t):
                key = (function.__name__, t)
                if key not in memo:
                    memo[key] = function(t)
                return memo[key]

            return call

        def wrapped(load, t):
            if t >= 0:
                return load(min(t, tiles - 1))
            return pltpu.roll(load(tiles - 1), LANES - rest, 1) if rest else load(tiles - 1)

        @cached
        def q(t):
            return wrapped(lambda k: tile_of(q_ref, p, k), t)

        @cached
        def q_left(t):
            return pltpu.roll(q(t), LANES - 1, 1)

        @cached
        def q_east(t):
            return jnp.where(lane == LANES - 1, q_left(min(t + 1, tiles - 1)), q_left(t))

        @cached
        def d(t):
            return q_east(t) - q(t)

        @cached
        def d_right(t):
            return pltpu.roll(d(t), 1, 1)

        @cached
        def s(t):
            return min_mod(d(t), jnp.where(lane == 0, d_right(max(t - 1, -1)), d_right(t)))

        @cached
        def s_left(t):
            return pltpu.roll(s(t), LANES - 1, 1)

        @cached
        def east(t):
            s_east = jnp.where(lane == LANES - 1, s_left(min(t + 1, tiles - 1)), s_left(t))
            c = wrapped(lambda k: tile_of(ce_ref, level, k), t)
            ch = wrapped(lambda k: che_s[level, :, LANES * k : LANES * (k + 1)], t)
            return upwind(c, ch, q(t), s(t), q_east(t), s_east)

        @cached
        def east_right(t):
            return pltpu.roll(east(t), 1, 1)

        rn, rs = ratio_ref[0], ratio_ref[1]
        for t in range(tiles):
            inc_x = jnp.where(lane == 0, east_right(t - 1), east_right(t)) - east(t)
            here = q(t)
            halo = tile_of(halo_ref, p, t)
            low0, low1, high0, high1 = (halo[k : k + 1] for k in range(4))
            cn = tile_of(cn_ref, level, t)
            chn = chn_s[level, :, LANES * t : LANES * (t + 1)]
            cs = tile_of(cs_ref, level, t)
            q_north = jnp.where(row == rows - 1, high0, pltpu.roll(here, rows - 1, 0))
            dy = q_north - here
            dy_low = here[0:1] - low1
            sy = min_mod(dy, jnp.where(row == 0, dy_low, pltpu.roll(dy, 1, 0)))
            sy_high = min_mod(high1 - high0, dy[rows - 1 : rows])
            sy_north = jnp.where(row == rows - 1, sy_high, pltpu.roll(sy, rows - 1, 0))
            north = upwind(cn, chn, here, sy, q_north, sy_north)
            sy_low = min_mod(dy_low, low1 - low0)
            south_row = upwind(cs, second(cs), low1, sy_low, here[0:1], sy[0:1])
            south = jnp.where(row == 0, south_row, pltpu.roll(north, 1, 0))
            put(t, here, inc_x + (rs * south - rn * north))

    @pl.when(jnp.logical_not(polar))
    def _():
        def plane(p, carry):
            def put(t, here, inc):
                size = LANES if t < full else rest
                out_ref[p, :, LANES * t : LANES * t + size] = (here + inc)[:, :size]

            increments(p, lax.rem(p, levels), put)
            return carry

        lax.fori_loop(0, planes, plane, 0)

    @pl.when(polar)
    def _():
        def plane(p, carry):
            def put(t, here, inc):
                if t >= full:
                    inc = jnp.where(lane < rest, inc, 0.0)
                inc_s[:, LANES * t : LANES * (t + 1)] = inc

            increments(p, lax.rem(p, levels), put)
            x0, x1, x2, x3 = (inc_s[:, part * k : part * k + deep] for k in range(4))
            a, b = x0 + x2, x1 + x3
            where = pl.ds(pl.multiple_of(p * rows, rows), rows)
            for k, y in enumerate((a + b, a - b, x0 - x2, x1 - x3)):
                y_s[where, deep * k : deep * (k + 1)] = y.astype(jnp.bfloat16)
            return carry

        lax.fori_loop(0, planes, plane, 0)
        total = planes * rows

        def forward(y, matrix, at):
            coefficients = jnp.dot(y, matrix, preferred_element_type=jnp.float32)
            scaled = coefficients.reshape(planes, rows, CHUNK) * resp_ref[:, at : at + CHUNK][None]
            s_s[:, at : at + CHUNK] = scaled.reshape(total, CHUNK).astype(jnp.bfloat16)

        copies[0].wait()
        for k in range(2):
            for n in range(deep // CHUNK):
                forward(
                    y_s[:, deep * k : deep * (k + 1)],
                    even_s[k, :, CHUNK * n : CHUNK * (n + 1)],
                    deep * k + CHUNK * n,
                )
        copies[1].wait()
        for n in range(2 * deep // CHUNK):
            forward(
                y_s[:, 2 * deep :], odd_s[:, CHUNK * n : CHUNK * (n + 1)], 2 * deep + CHUNK * n
            )
        copies[2].wait()
        copies[3].wait()
        for n in range(deep // CHUNK):
            span = slice(CHUNK * n, CHUNK * (n + 1))
            size = min(CHUNK, part - CHUNK * n)

            def back(scaled, matrix):
                return jnp.dot(scaled, matrix, preferred_element_type=jnp.float32)

            e0 = back(s_s[:, :deep], even_t_s[0, :, span])
            e2 = back(s_s[:, deep : 2 * deep], even_t_s[1, :, span])
            eu = back(s_s[:, 2 * deep :], odd_t_s[:, span])
            ev = back(s_s[:, 2 * deep :], odd_t_s[:, deep + CHUNK * n : deep + CHUNK * (n + 1)])
            plus, minus = e0 + e2, e0 - e2
            for k, value in enumerate((plus + eu, minus + ev, plus - eu, minus - ev)):
                start = part * k + CHUNK * n
                out_ref[:, :, start : start + size] = (
                    q_ref[:, :, start : start + size]
                    + value.reshape(planes, rows, CHUNK)[:, :, :size]
                )


def shifted(x, axis, by):
    count = lax.axis_size(axis)
    return lax.ppermute(x, axis, [(i, i + by) for i in range(count) if 0 <= i + by < count])


def on_device(tracers, east_courant, north_courant, spectrum, filter_index):
    fields, levels, rows, width = tracers.shape
    planes = fields * levels
    devices = lax.axis_size("lon")
    device = lax.axis_index("lon")
    part = width // 4
    deep = up_to(part, CHUNK)
    wide = up_to(width, LANES)
    q = tracers.reshape(planes, rows, width)
    kind = jnp.bfloat16
    up = jnp.concatenate(
        [
            q[:, rows - 2 :].astype(kind).reshape(2 * planes, width),
            north_courant[:, rows - 1].astype(kind),
        ],
        axis=0,
    )
    low = shifted(up, "lon", 1)
    high = shifted(q[:, :2].astype(kind).reshape(2 * planes, width), "lon", -1)
    halo = jnp.concatenate(
        [low[: 2 * planes].reshape(planes, 2, width), high.reshape(planes, 2, width)], axis=1
    ).astype(jnp.float32)
    south_courant = low[2 * planes :].astype(jnp.float32).reshape(levels, 1, width)
    spacing = math.pi / (rows * devices)
    where = (device * rows + jnp.arange(rows, dtype=jnp.int32)).astype(jnp.float32)
    center = jnp.sin((where + 0.5) * spacing)
    ratio = jnp.stack([jnp.sin((where + 1.0) * spacing) / center, jnp.sin(where * spacing) / center])
    ratio = jnp.broadcast_to(ratio[:, :, None], (2, rows, LANES))
    quarter = devices // 4
    polar = ((device < quarter) | (device >= devices - quarter)).astype(jnp.int32).reshape(1)
    half = width // 2
    chosen = jnp.take(spectrum, lax.dynamic_slice_in_dim(filter_index, device * rows, rows), axis=0)
    column = np.arange(width)
    weight = np.where((column == 0) | (column == half), 1.0 / width, 2.0 / width).astype(np.float32)
    chosen = chosen * weight[None, :]
    zeros = jnp.zeros((rows, deep - part), jnp.float32)
    response = jnp.concatenate(
        [
            chosen[:, 0 : half + 1 : 4], chosen[:, half + 4 :: 4], zeros,
            chosen[:, 2 : half + 1 : 4], chosen[:, half + 2 :: 4], zeros,
            chosen[:, 1 : half + 1 : 2], chosen[:, half + 1 :: 2], zeros, zeros,
        ],
        axis=1,
    )
    matrices = [jnp.asarray(m) for m in make_matrices(width)]
    vmem = pl.BlockSpec(memory_space=pltpu.VMEM)
    out = pl.pallas_call(
        functools.partial(kernel, width),
        out_shape=jax.ShapeDtypeStruct(q.shape, jnp.float32),
        in_specs=[pl.BlockSpec(memory_space=pltpu.SMEM)] + [vmem] * 7 + [pl.BlockSpec(memory_space=pl.ANY)] * 4,
        out_specs=vmem,
        scratch_shapes=[
            pltpu.VMEM((levels, rows, wide), jnp.float32),
            pltpu.VMEM((levels, rows, wide), jnp.float32),
            pltpu.VMEM((rows, 3 * part + deep + LANES), jnp.float32),
            pltpu.VMEM((planes * rows, 4 * deep), kind),
            pltpu.VMEM((planes * rows, 4 * deep), kind),
        ]
        + [pltpu.VMEM(m.shape, kind) for m in matrices]
        + [pltpu.SemaphoreType.DMA((4,))],
        compiler_params=pltpu.CompilerParams(vmem_limit_bytes=56 * 2**20),
    )(polar, q, east_courant, north_courant, south_courant, halo, ratio, response, *matrices)
    return out.reshape(tracers.shape)


def solution(mesh):
    placed = (P("grp", None, "lon", None), P("grp", "lon", None), P("grp", "lon", None), P(), P())
    return jax.shard_map(
        on_device,
        mesh=mesh,
        in_specs=placed,
        out_specs=P("grp", None, "lon", None),
        check_vma=False,
    )
```

```python
import functools
import math

import jax
import jax.numpy as jnp
import ml_dtypes
import numpy as np
from jax import lax
from jax.experimental import pallas as pl
from jax.experimental.pallas import tpu as pltpu
from jax.sharding import PartitionSpec as P

LANES = 128
CHUNK = 256


def up_to(value, multiple):
    return -(-value // multiple) * multiple


def column_groups(width):
    half = width // 2
    column = np.arange(width)
    number = np.where(column <= half, column, column - half)
    return number, [np.where(number % 4 == 0)[0], np.where(number % 4 == 2)[0], np.where(number % 2 == 1)[0]]


def make_matrices(width):
    half, part = width // 2, width // 4
    deep = up_to(part, CHUNK)
    number, groups = column_groups(width)
    points = np.arange(half, dtype=np.int64)[:, None]
    angle = ((points * number[None, :]) % width) * (2.0 * math.pi / width)
    basis = np.where(np.arange(width)[None, :] <= half, np.cos(angle), np.sin(angle))
    even = np.zeros((2, deep, deep), np.float64)
    for at in range(2):
        even[at, :part, : len(groups[at])] = basis[:part, groups[at]]
    odd = np.zeros((2, deep, 2 * deep), np.float64)
    odd[0, :part, : len(groups[2])] = basis[:part, groups[2]]
    odd[1, :part, : len(groups[2])] = basis[part:, groups[2]]
    odd = odd.reshape(2 * deep, 2 * deep)
    kind = ml_dtypes.bfloat16
    return (
        even.astype(kind),
        odd.astype(kind),
        np.ascontiguousarray(even.transpose(0, 2, 1)).astype(kind),
        np.ascontiguousarray(odd.T).astype(kind),
    )


def make_order():
    at = np.arange(CHUNK)
    source = np.concatenate([at[at % 4 == 0], at[at % 4 == 2], at[at % 2 == 1]])
    order = np.zeros((CHUNK, CHUNK), np.float32)
    order[source, at] = 1.0
    return order.astype(ml_dtypes.bfloat16)


def exchange(count, q_hbm, cn_hbm, edge_ref, south_s, north_s, cn_s, packs, up_s, down_s, low_s, high_s,
             local, send, recv):
    planes, rows, width = q_hbm.shape
    levels = cn_hbm.shape[0]
    deep = edge_ref.shape[1]
    me = lax.axis_index("lon")
    last = count - 1
    loads = [
        pltpu.make_async_copy(q_hbm.at[:, pl.ds(rows - 8, 8), :], north_s, local.at[0]),
        pltpu.make_async_copy(cn_hbm.at[:, pl.ds(rows - 8, 8), :], cn_s, local.at[1]),
        pltpu.make_async_copy(q_hbm.at[:, pl.ds(0, 8), :], south_s, local.at[2]),
    ]
    for load in loads:
        load.start()
    barrier = pltpu.get_barrier_semaphore()

    @pl.when(me > 0)
    def _():
        pl.semaphore_signal(barrier, inc=1, device_id={"lon": me - 1}, device_id_type=pl.DeviceIdType.MESH)

    @pl.when(me < last)
    def _():
        pl.semaphore_signal(barrier, inc=1, device_id={"lon": me + 1}, device_id_type=pl.DeviceIdType.MESH)

    for at in range(2):
        packs[at, 2 * deep - levels :, :] = jnp.zeros((levels, width), jnp.float32)
        packs[at, planes:deep, :] = jnp.zeros((levels, width), jnp.float32)

    loads[0].wait()
    loads[1].wait()
    for p in range(planes):
        packs[0, p : p + 1, :] = north_s[p, 6:7, :]
        packs[0, deep + p : deep + p + 1, :] = north_s[p, 7:8, :]
    for p in range(levels):
        packs[0, planes + p : planes + p + 1, :] = cn_s[p, 7:8, :]
    up_s[...] = packs[0].astype(jnp.bfloat16)

    outer = jnp.logical_or(me == 0, me == last)

    @pl.when(outer)
    def _():
        pl.semaphore_wait(barrier, 1)

    @pl.when(jnp.logical_not(outer))
    def _():
        pl.semaphore_wait(barrier, 2)

    up = pltpu.make_async_remote_copy(
        src_ref=up_s, dst_ref=low_s, send_sem=send.at[0], recv_sem=recv.at[0],
        device_id={"lon": me + 1}, device_id_type=pl.DeviceIdType.MESH,
    )
    down = pltpu.make_async_remote_copy(
        src_ref=down_s, dst_ref=high_s, send_sem=send.at[1], recv_sem=recv.at[1],
        device_id={"lon": me - 1}, device_id_type=pl.DeviceIdType.MESH,
    )

    @pl.when(me < last)
    def _():
        up.start()

    loads[2].wait()
    for p in range(planes):
        packs[1, p : p + 1, :] = south_s[p, 0:1, :]
        packs[1, deep + p : deep + p + 1, :] = south_s[p, 1:2, :]
    down_s[...] = packs[1].astype(jnp.bfloat16)

    @pl.when(me > 0)
    def _():
        down.start()
        up.wait_recv()

    @pl.when(me == 0)
    def _():
        low_s[...] = jnp.zeros_like(low_s)

    @pl.when(me < last)
    def _():
        down.wait_recv()

    @pl.when(me == last)
    def _():
        high_s[...] = jnp.zeros_like(high_s)

    for start in range(0, width, LANES):
        span = slice(start, min(start + LANES, width))
        low = low_s[:, span].astype(jnp.float32)
        high = high_s[:, span].astype(jnp.float32)
        low0, low1, high0, high1 = low[:deep], low[deep:], high[:deep], high[deep:]
        q0, q1, q_last = packs[1, :deep, span], packs[1, deep:, span], packs[0, deep:, span]
        cs = jnp.concatenate([low[planes : planes + levels]] * (deep // levels), axis=0)
        dy = q0 - low1
        edge_ref[0, :, span] = upwind(
            cs, second(cs), low1, min_mod(dy, low1 - low0), q0, min_mod(q1 - q0, dy)
        )
        edge_ref[1, :, span] = high0
        edge_ref[2, :, span] = min_mod(high1 - high0, high0 - q_last)
        edge_ref[3, :, span] = low1

    @pl.when(me < last)
    def _():
        up.wait_send()

    @pl.when(me > 0)
    def _():
        down.wait_send()


def min_mod(a, b):
    return jnp.maximum(jnp.minimum(a, jnp.maximum(b, 0.0)), jnp.minimum(b, 0.0))


def upwind(c, ch, ql, sl, qr, sr):
    ahead = c > 0.0
    return c * jnp.where(ahead, ql, qr) + ch * jnp.where(ahead, sl, sr)


def second(c):
    return c * (jnp.where(c > 0.0, 0.5, -0.5) - 0.5 * c)


def kernel(width, count, where_ref, index_ref, q_hbm, ce_ref, cn_ref, edge_ref, spectrum_ref, order_ref,
           even_hbm, odd_hbm, even_t_hbm, odd_t_hbm, out_hbm,
           q_ref, out_ref, chosen_s, resp_ref, ratio_s, che_s, chn_s, inc_s, y_s, s_s,
           even_s, odd_s, even_t_s, odd_t_s, sems, in_sems, out_sems):
    planes, rows, _ = q_ref.shape
    levels = ce_ref.shape[0]
    part = width // 4
    deep = up_to(part, CHUNK)
    full = width // LANES
    rest = width - full * LANES
    tiles = full + (1 if rest else 0)
    lane = lax.broadcasted_iota(jnp.int32, (rows, LANES), 1)
    row = lax.broadcasted_iota(jnp.int32, (rows, LANES), 0)
    copies = [
        pltpu.make_async_copy(source, target, sems.at[at])
        for at, (source, target) in enumerate(
            ((even_hbm, even_s), (odd_hbm, odd_s), (even_t_hbm, even_t_s), (odd_t_hbm, odd_t_s))
        )
    ]
    device = where_ref[0]
    quarter = count // 4
    polar = jnp.logical_or(device < quarter, device >= count - quarter)

    def q_copy(p):
        return pltpu.make_async_copy(q_hbm.at[p], q_ref.at[p], in_sems.at[p])

    def out_copy(p):
        return pltpu.make_async_copy(out_ref.at[p], out_hbm.at[p], out_sems.at[p])

    def over_planes(act):
        lax.fori_loop(0, planes, lambda p, carry: (act(p), carry)[1], 0)

    over_planes(lambda p: q_copy(p).start())

    @pl.when(polar)
    def _():
        for copy in copies:
            copy.start()

    spacing = math.pi / (rows * count)
    place = (device * rows + row).astype(jnp.float32)
    center = jnp.sin((place + 0.5) * spacing)
    ratio_s[0] = jnp.sin((place + 1.0) * spacing) / center
    ratio_s[1] = jnp.sin(place * spacing) / center

    def tile_of(ref, at, t):
        if t < full:
            return ref[at, :, LANES * t : LANES * (t + 1)]
        return jnp.concatenate(
            [ref[at, :, LANES * full : width], ref[at, :, : LANES - rest]], axis=1
        )

    def prepare(level, carry):
        for t in range(tiles):
            che_s[level, :, LANES * t : LANES * (t + 1)] = second(tile_of(ce_ref, level, t))
            chn_s[level, :, LANES * t : LANES * (t + 1)] = second(tile_of(cn_ref, level, t))
        return carry

    lax.fori_loop(0, levels, prepare, 0)

    def increments(p, level, put):
        memo = {}

        def cached(function):
            def call(t):
                key = (function.__name__, t)
                if key not in memo:
                    memo[key] = function(t)
                return memo[key]

            return call

        def wrapped(load, t):
            if t >= 0:
                return load(min(t, tiles - 1))
            return pltpu.roll(load(tiles - 1), LANES - rest, 1) if rest else load(tiles - 1)

        @cached
        def q(t):
            return wrapped(lambda k: tile_of(q_ref, p, k), t)

        @cached
        def q_left(t):
            return pltpu.roll(q(t), LANES - 1, 1)

        @cached
        def q_east(t):
            return jnp.where(lane == LANES - 1, q_left(min(t + 1, tiles - 1)), q_left(t))

        @cached
        def d(t):
            return q_east(t) - q(t)

        @cached
        def d_right(t):
            return pltpu.roll(d(t), 1, 1)

        @cached
        def s(t):
            return min_mod(d(t), jnp.where(lane == 0, d_right(max(t - 1, -1)), d_right(t)))

        @cached
        def s_left(t):
            return pltpu.roll(s(t), LANES - 1, 1)

        @cached
        def east(t):
            s_east = jnp.where(lane == LANES - 1, s_left(min(t + 1, tiles - 1)), s_left(t))
            c = wrapped(lambda k: tile_of(ce_ref, level, k), t)
            ch = wrapped(lambda k: che_s[level, :, LANES * k : LANES * (k + 1)], t)
            return upwind(c, ch, q(t), s(t), q_east(t), s_east)

        @cached
        def east_right(t):
            return pltpu.roll(east(t), 1, 1)

        rn, rs = ratio_s[0], ratio_s[1]

        def edge(k, t, target):
            at = pl.ds(pl.multiple_of(p // 8 * 8, 8), 8)
            if t < full:
                value = edge_ref[k, at, LANES * t : LANES * (t + 1)]
            else:
                value = jnp.concatenate(
                    [edge_ref[k, at, LANES * full : width], edge_ref[k, at, : LANES - rest]], axis=1
                )
            value = pltpu.roll(value, lax.rem(target + 8 - lax.rem(p, 8), 8), 0)
            return jnp.concatenate([value] * (rows // 8), axis=0)

        for t in range(tiles):
            inc_x = jnp.where(lane == 0, east_right(t - 1), east_right(t)) - east(t)
            here = q(t)
            cn = tile_of(cn_ref, level, t)
            chn = chn_s[level, :, LANES * t : LANES * (t + 1)]
            q_north = jnp.where(row == rows - 1, edge(1, t, 7), pltpu.roll(here, rows - 1, 0))
            dy = q_north - here
            dy_south = jnp.where(row == 0, here - edge(3, t, 0), pltpu.roll(dy, 1, 0))
            sy = min_mod(dy, dy_south)
            sy_north = jnp.where(row == rows - 1, edge(2, t, 7), pltpu.roll(sy, rows - 1, 0))
            north = upwind(cn, chn, here, sy, q_north, sy_north)
            south = jnp.where(row == 0, edge(0, t, 0), pltpu.roll(north, 1, 0))
            put(t, here, inc_x + (rs * south - rn * north))

    def respond():
        half = width // 2
        filters = spectrum_ref.shape[0]
        spot = lax.broadcasted_iota(jnp.int32, (rows, filters), 0)
        picked = jnp.zeros((rows, filters), jnp.int32)
        for j in range(rows):
            picked = jnp.where(spot == j, index_ref[device * rows + j], picked)
        one_hot = picked == lax.broadcasted_iota(jnp.int32, (rows, filters), 1)
        one_hot = one_hot.astype(jnp.float32).astype(jnp.bfloat16)
        for start in range(0, width, 2 * CHUNK):
            span = slice(start, min(start + 2 * CHUNK, width))
            value = spectrum_ref[:, span]
            chosen = jnp.zeros((rows, span.stop - start), jnp.float32)
            for _ in range(3):
                piece = value.astype(jnp.bfloat16)
                chosen = chosen + jnp.dot(one_hot, piece, preferred_element_type=jnp.float32)
                value = value - piece.astype(jnp.float32)
            chosen_s[:, span] = chosen
        blocks = 4 * deep // CHUNK
        chosen_s[:, width:] = jnp.zeros((rows, CHUNK * blocks - width), jnp.float32)
        column = lax.broadcasted_iota(jnp.int32, (rows, CHUNK), 1)
        parts = []
        for b in range(blocks):
            here = column + CHUNK * b
            weight = jnp.where((here == 0) | (here == half), 1.0 / width, 2.0 / width)
            value = chosen_s[:, CHUNK * b : CHUNK * (b + 1)] * weight
            for _ in range(3):
                piece = value.astype(jnp.bfloat16)
                parts.append(piece)
                value = value - piece.astype(jnp.float32)
        moved = jnp.dot(jnp.concatenate(parts, axis=0), order_ref[...], preferred_element_type=jnp.float32)
        moved = moved.reshape(blocks, 3, rows, CHUNK)
        moved = moved[:, 0] + moved[:, 1] + moved[:, 2]
        low_half = lane < LANES // 2
        for b in range(blocks):
            at = 2 * deep + LANES * b
            resp_ref[:, at : at + LANES] = moved[b, :, LANES:]
        for b in range(0, blocks, 2):
            at = LANES // 2 * b
            a, c = moved[b, :, :LANES], moved[b + 1, :, :LANES]
            resp_ref[:, at : at + LANES] = jnp.where(low_half, a, pltpu.roll(c, LANES // 2, 1))
            resp_ref[:, deep + at : deep + at + LANES] = jnp.where(
                low_half, pltpu.roll(a, LANES // 2, 1), c
            )

    @pl.when(jnp.logical_not(polar))
    def _():
        def plane(p, carry):
            def put(t, here, inc):
                size = LANES if t < full else rest
                out_ref[p, :, LANES * t : LANES * t + size] = (here + inc)[:, :size]

            q_copy(p).wait()
            increments(p, lax.rem(p, levels), put)
            out_copy(p).start()
            return carry

        lax.fori_loop(0, planes, plane, 0)

    @pl.when(polar)
    def _():
        def plane(p, carry):
            def put(t, here, inc):
                if t >= full:
                    inc = jnp.where(lane < rest, inc, 0.0)
                inc_s[:, LANES * t : LANES * (t + 1)] = inc

            q_copy(p).wait()
            increments(p, lax.rem(p, levels), put)
            x0, x1, x2, x3 = (inc_s[:, part * k : part * k + deep] for k in range(4))
            a, b = x0 + x2, x1 + x3
            where = pl.ds(pl.multiple_of(p * rows, rows), rows)
            for k, y in enumerate((a + b, a - b, x0 - x2, x1 - x3)):
                y_s[where, deep * k : deep * (k + 1)] = y.astype(jnp.bfloat16)
            return carry

        lax.fori_loop(0, planes, plane, 0)
        total = planes * rows
        respond()

        def forward(y, matrix, at):
            coefficients = jnp.dot(y, matrix, preferred_element_type=jnp.float32)
            scaled = coefficients.reshape(planes, rows, CHUNK) * resp_ref[:, at : at + CHUNK][None]
            s_s[:, at : at + CHUNK] = scaled.reshape(total, CHUNK).astype(jnp.bfloat16)

        copies[0].wait()
        for k in range(2):
            for n in range(deep // CHUNK):
                forward(
                    y_s[:, deep * k : deep * (k + 1)],
                    even_s[k, :, CHUNK * n : CHUNK * (n + 1)],
                    deep * k + CHUNK * n,
                )
        copies[1].wait()
        for n in range(2 * deep // CHUNK):
            forward(
                y_s[:, 2 * deep :], odd_s[:, CHUNK * n : CHUNK * (n + 1)], 2 * deep + CHUNK * n
            )
        copies[2].wait()
        copies[3].wait()
        for n in range(deep // CHUNK):
            span = slice(CHUNK * n, CHUNK * (n + 1))
            size = min(CHUNK, part - CHUNK * n)

            def back(scaled, matrix):
                return jnp.dot(scaled, matrix, preferred_element_type=jnp.float32)

            e0 = back(s_s[:, :deep], even_t_s[0, :, span])
            e2 = back(s_s[:, deep : 2 * deep], even_t_s[1, :, span])
            eu = back(s_s[:, 2 * deep :], odd_t_s[:, span])
            ev = back(s_s[:, 2 * deep :], odd_t_s[:, deep + CHUNK * n : deep + CHUNK * (n + 1)])
            plus, minus = e0 + e2, e0 - e2
            for k, value in enumerate((plus + eu, minus + ev, plus - eu, minus - ev)):
                start = part * k + CHUNK * n
                out_ref[:, :, start : start + size] = (
                    q_ref[:, :, start : start + size]
                    + value.reshape(planes, rows, CHUNK)[:, :, :size]
                )
        over_planes(lambda p: out_copy(p).start())

    over_planes(lambda p: out_copy(p).wait())


def on_device(tracers, east_courant, north_courant, spectrum, filter_index):
    fields, levels, rows, width = tracers.shape
    planes = fields * levels
    devices = lax.axis_size("lon")
    device = lax.axis_index("lon")
    part = width // 4
    deep = up_to(part, CHUNK)
    wide = up_to(width, LANES)
    stacked = up_to(planes + levels, 8)
    q = tracers.reshape(planes, rows, width)
    kind = jnp.bfloat16
    vmem = pl.BlockSpec(memory_space=pltpu.VMEM)
    smem = pl.BlockSpec(memory_space=pltpu.SMEM)
    anywhere = pl.BlockSpec(memory_space=pl.ANY)
    edge = pl.pallas_call(
        functools.partial(exchange, devices),
        out_shape=jax.ShapeDtypeStruct((4, stacked, width), jnp.float32),
        in_specs=[anywhere] * 2,
        out_specs=vmem,
        scratch_shapes=[
            pltpu.VMEM((planes, 8, width), jnp.float32),
            pltpu.VMEM((planes, 8, width), jnp.float32),
            pltpu.VMEM((levels, 8, width), jnp.float32),
            pltpu.VMEM((2, 2 * stacked, width), jnp.float32),
        ]
        + [pltpu.VMEM((2 * stacked, width), kind)] * 4
        + [pltpu.SemaphoreType.DMA((3,)), pltpu.SemaphoreType.DMA((2,)), pltpu.SemaphoreType.DMA((2,))],
        compiler_params=pltpu.CompilerParams(
            collective_id=0, has_side_effects=True, vmem_limit_bytes=56 * 2**20
        ),
    )(q, north_courant)
    matrices = [jnp.asarray(m) for m in make_matrices(width)]
    out = pl.pallas_call(
        functools.partial(kernel, width, devices),
        out_shape=jax.ShapeDtypeStruct(q.shape, jnp.float32),
        in_specs=[smem, smem, anywhere] + [vmem] * 5 + [anywhere] * 4,
        out_specs=anywhere,
        scratch_shapes=[
            pltpu.VMEM((planes, rows, width), jnp.float32),
            pltpu.VMEM((planes, rows, width), jnp.float32),
            pltpu.VMEM((rows, 4 * deep), jnp.float32),
            pltpu.VMEM((rows, 4 * deep), jnp.float32),
            pltpu.VMEM((2, rows, LANES), jnp.float32),
            pltpu.VMEM((levels, rows, wide), jnp.float32),
            pltpu.VMEM((levels, rows, wide), jnp.float32),
            pltpu.VMEM((rows, 3 * part + deep + LANES), jnp.float32),
            pltpu.VMEM((planes * rows, 4 * deep), kind),
            pltpu.VMEM((planes * rows, 4 * deep), kind),
        ]
        + [pltpu.VMEM(m.shape, kind) for m in matrices]
        + [pltpu.SemaphoreType.DMA((n,)) for n in (4, planes, planes)],
        compiler_params=pltpu.CompilerParams(vmem_limit_bytes=56 * 2**20),
    )(
        device.astype(jnp.int32).reshape(1), filter_index, q, east_courant, north_courant, edge,
        spectrum, jnp.asarray(make_order()), *matrices,
    )
    return out.reshape(tracers.shape)


def solution(mesh):
    placed = (P("grp", None, "lon", None), P("grp", "lon", None), P("grp", "lon", None), P(), P())
    return jax.shard_map(
        on_device,
        mesh=mesh,
        in_specs=placed,
        out_specs=P("grp", None, "lon", None),
        check_vma=False,
    )
```

```python
import functools
import math

import jax
import jax.numpy as jnp
import ml_dtypes
import numpy as np
from jax import lax
from jax.experimental import pallas as pl
from jax.experimental.pallas import tpu as pltpu
from jax.sharding import PartitionSpec as P

LANES = 128
CHUNK = 256


def up_to(value, multiple):
    return -(-value // multiple) * multiple


def column_groups(width):
    half = width // 2
    column = np.arange(width)
    number = np.where(column <= half, column, column - half)
    return number, [np.where(number % 4 == 0)[0], np.where(number % 4 == 2)[0], np.where(number % 2 == 1)[0]]


def make_matrices(width):
    half, part = width // 2, width // 4
    deep = up_to(part, CHUNK)
    number, groups = column_groups(width)
    points = np.arange(half, dtype=np.int64)[:, None]
    angle = ((points * number[None, :]) % width) * (2.0 * math.pi / width)
    basis = np.where(np.arange(width)[None, :] <= half, np.cos(angle), np.sin(angle))
    even = np.zeros((2, deep, deep), np.float64)
    for at in range(2):
        even[at, :part, : len(groups[at])] = basis[:part, groups[at]]
    odd = np.zeros((2, deep, 2 * deep), np.float64)
    odd[0, :part, : len(groups[2])] = basis[:part, groups[2]]
    odd[1, :part, : len(groups[2])] = basis[part:, groups[2]]
    odd = odd.reshape(2 * deep, 2 * deep)
    kind = ml_dtypes.bfloat16
    return (
        even.astype(kind),
        odd.astype(kind),
        np.ascontiguousarray(even.transpose(0, 2, 1)).astype(kind),
        np.ascontiguousarray(odd.T).astype(kind),
    )


def make_order():
    at = np.arange(CHUNK)
    source = np.concatenate([at[at % 4 == 0], at[at % 4 == 2], at[at % 2 == 1]])
    order = np.zeros((CHUNK, CHUNK), np.float32)
    order[source, at] = 1.0
    return order.astype(ml_dtypes.bfloat16)


def tile_of(ref, at, t):
    width = ref.shape[-1]
    if LANES * (t + 1) <= width:
        return ref[at, :, LANES * t : LANES * (t + 1)]
    start = LANES * t
    return jnp.concatenate([ref[at, :, start:width], ref[at, :, : start + LANES - width]], axis=1)


def east_west(width, rows, load_q, load_c, load_ch, put):
    tiles = -(-width // LANES)
    rest = width % LANES
    lane = lax.broadcasted_iota(jnp.int32, (rows, LANES), 1)
    memo = {}

    def cached(function):
        def call(t):
            key = (function.__name__, t)
            if key not in memo:
                memo[key] = function(t)
            return memo[key]

        return call

    def wrapped(load, t):
        if t >= 0:
            return load(min(t, tiles - 1))
        return pltpu.roll(load(tiles - 1), LANES - rest, 1) if rest else load(tiles - 1)

    @cached
    def q(t):
        return wrapped(load_q, t)

    @cached
    def q_left(t):
        return pltpu.roll(q(t), LANES - 1, 1)

    @cached
    def q_east(t):
        return jnp.where(lane == LANES - 1, q_left(min(t + 1, tiles - 1)), q_left(t))

    @cached
    def d(t):
        return q_east(t) - q(t)

    @cached
    def d_right(t):
        return pltpu.roll(d(t), 1, 1)

    @cached
    def s(t):
        return min_mod(d(t), jnp.where(lane == 0, d_right(max(t - 1, -1)), d_right(t)))

    @cached
    def s_left(t):
        return pltpu.roll(s(t), LANES - 1, 1)

    @cached
    def east(t):
        s_east = jnp.where(lane == LANES - 1, s_left(min(t + 1, tiles - 1)), s_left(t))
        c = wrapped(load_c, t)
        ch = wrapped(load_ch, t)
        return upwind(c, ch, q(t), s(t), q_east(t), s_east)

    @cached
    def east_right(t):
        return pltpu.roll(east(t), 1, 1)

    for t in range(tiles):
        put(t, jnp.where(lane == 0, east_right(t - 1), east_right(t)) - east(t))


def exchange(count, q_hbm, ce_hbm, cn_hbm, edge_ref, x_hbm, south_s, north_s, cn_s, ce_s, che_s, x_s, packs, up_s, down_s, low_s, high_s,
             local, send, recv, x_sems):
    planes, rows, width = q_hbm.shape
    levels = cn_hbm.shape[0]
    deep = edge_ref.shape[1]
    me = lax.axis_index("lon")
    last = count - 1
    loads = [
        pltpu.make_async_copy(q_hbm.at[:, pl.ds(rows - 8, 8), :], north_s, local.at[0]),
        pltpu.make_async_copy(cn_hbm.at[:, pl.ds(rows - 8, 8), :], cn_s, local.at[1]),
        pltpu.make_async_copy(q_hbm.at[:, pl.ds(0, 8), :], south_s, local.at[2]),
        pltpu.make_async_copy(ce_hbm, ce_s, local.at[3]),
    ]
    for load in loads:
        load.start()
    barrier = pltpu.get_barrier_semaphore()

    @pl.when(me > 0)
    def _():
        pl.semaphore_signal(barrier, inc=1, device_id={"lon": me - 1}, device_id_type=pl.DeviceIdType.MESH)

    @pl.when(me < last)
    def _():
        pl.semaphore_signal(barrier, inc=1, device_id={"lon": me + 1}, device_id_type=pl.DeviceIdType.MESH)

    for at in range(2):
        packs[at, 2 * deep - levels :, :] = jnp.zeros((levels, width), jnp.float32)
        packs[at, planes:deep, :] = jnp.zeros((levels, width), jnp.float32)

    loads[0].wait()
    loads[1].wait()
    for p in range(planes):
        packs[0, p : p + 1, :] = north_s[p, 6:7, :]
        packs[0, deep + p : deep + p + 1, :] = north_s[p, 7:8, :]
    for p in range(levels):
        packs[0, planes + p : planes + p + 1, :] = cn_s[p, 7:8, :]
    up_s[...] = packs[0].astype(jnp.bfloat16)

    outer = jnp.logical_or(me == 0, me == last)

    @pl.when(outer)
    def _():
        pl.semaphore_wait(barrier, 1)

    @pl.when(jnp.logical_not(outer))
    def _():
        pl.semaphore_wait(barrier, 2)

    up = pltpu.make_async_remote_copy(
        src_ref=up_s, dst_ref=low_s, send_sem=send.at[0], recv_sem=recv.at[0],
        device_id={"lon": me + 1}, device_id_type=pl.DeviceIdType.MESH,
    )
    down = pltpu.make_async_remote_copy(
        src_ref=down_s, dst_ref=high_s, send_sem=send.at[1], recv_sem=recv.at[1],
        device_id={"lon": me - 1}, device_id_type=pl.DeviceIdType.MESH,
    )

    @pl.when(me < last)
    def _():
        up.start()

    loads[2].wait()
    for p in range(planes):
        packs[1, p : p + 1, :] = south_s[p, 0:1, :]
        packs[1, deep + p : deep + p + 1, :] = south_s[p, 1:2, :]
    down_s[...] = packs[1].astype(jnp.bfloat16)

    @pl.when(me > 0)
    def _():
        down.start()

    loads[3].wait()
    tiles = -(-width // LANES)

    def prepare(level, carry):
        for t in range(tiles):
            che_s[level, :, LANES * t : LANES * (t + 1)] = second(tile_of(ce_s, level, t))
        return carry

    lax.fori_loop(0, levels, prepare, 0)

    def x_copy(p):
        return pltpu.make_async_copy(x_s.at[p], x_hbm.at[p], x_sems.at[p])

    def plane(p, carry):
        level = lax.rem(p, levels)

        def put(t, value):
            size = min(LANES, width - LANES * t)
            x_s[p, :, LANES * t : LANES * t + size] = value[:, :size]

        def load_q(t):
            return jnp.concatenate([tile_of(south_s, p, t), tile_of(north_s, p, t)], axis=0)

        east_west(
            width, rows, load_q, lambda t: tile_of(ce_s, level, t),
            lambda t: che_s[level, :, LANES * t : LANES * (t + 1)], put,
        )
        x_copy(p).start()
        return carry

    lax.fori_loop(0, planes, plane, 0)

    @pl.when(me > 0)
    def _():
        up.wait_recv()

    @pl.when(me == 0)
    def _():
        low_s[...] = jnp.zeros_like(low_s)

    @pl.when(me < last)
    def _():
        down.wait_recv()

    @pl.when(me == last)
    def _():
        high_s[...] = jnp.zeros_like(high_s)

    for start in range(0, width, LANES):
        span = slice(start, min(start + LANES, width))
        low = low_s[:, span].astype(jnp.float32)
        high = high_s[:, span].astype(jnp.float32)
        low0, low1, high0, high1 = low[:deep], low[deep:], high[:deep], high[deep:]
        q0, q1, q_last = packs[1, :deep, span], packs[1, deep:, span], packs[0, deep:, span]
        cs = jnp.concatenate([low[planes : planes + levels]] * (deep // levels), axis=0)
        dy = q0 - low1
        edge_ref[0, :, span] = upwind(
            cs, second(cs), low1, min_mod(dy, low1 - low0), q0, min_mod(q1 - q0, dy)
        )
        edge_ref[1, :, span] = high0
        edge_ref[2, :, span] = min_mod(high1 - high0, high0 - q_last)
        edge_ref[3, :, span] = low1

    @pl.when(me < last)
    def _():
        up.wait_send()

    @pl.when(me > 0)
    def _():
        down.wait_send()

    def finish(p, carry):
        x_copy(p).wait()
        return carry

    lax.fori_loop(0, planes, finish, 0)


def min_mod(a, b):
    return jnp.maximum(jnp.minimum(a, jnp.maximum(b, 0.0)), jnp.minimum(b, 0.0))


def upwind(c, ch, ql, sl, qr, sr):
    ahead = c > 0.0
    return c * jnp.where(ahead, ql, qr) + ch * jnp.where(ahead, sl, sr)


def second(c):
    return c * (jnp.where(c > 0.0, 0.5, -0.5) - 0.5 * c)


def kernel(width, count, where_ref, index_ref, q_hbm, x_hbm, cn_ref, edge_ref, spectrum_ref, order_ref,
           even_hbm, odd_hbm, even_t_hbm, odd_t_hbm, out_hbm,
           q_ref, x_ref, out_ref, chosen_s, resp_ref, ratio_s, chn_s, inc_s, y_s, s_s,
           even_s, odd_s, even_t_s, odd_t_s, sems, in_sems, x_sems, out_sems):
    planes, rows, _ = q_ref.shape
    levels = cn_ref.shape[0]
    part = width // 4
    deep = up_to(part, CHUNK)
    full = width // LANES
    rest = width - full * LANES
    tiles = full + (1 if rest else 0)
    lane = lax.broadcasted_iota(jnp.int32, (rows, LANES), 1)
    row = lax.broadcasted_iota(jnp.int32, (rows, LANES), 0)
    copies = [
        pltpu.make_async_copy(source, target, sems.at[at])
        for at, (source, target) in enumerate(
            ((even_hbm, even_s), (odd_hbm, odd_s), (even_t_hbm, even_t_s), (odd_t_hbm, odd_t_s))
        )
    ]
    device = where_ref[0]
    quarter = count // 4
    polar = jnp.logical_or(device < quarter, device >= count - quarter)

    def q_copy(p):
        return pltpu.make_async_copy(q_hbm.at[p], q_ref.at[p], in_sems.at[p])

    def x_copy(p):
        return pltpu.make_async_copy(x_hbm.at[p], x_ref.at[p], x_sems.at[p])

    def out_copy(p):
        return pltpu.make_async_copy(out_ref.at[p], out_hbm.at[p], out_sems.at[p])

    def over_planes(act):
        lax.fori_loop(0, planes, lambda p, carry: (act(p), carry)[1], 0)

    over_planes(lambda p: q_copy(p).start())
    over_planes(lambda p: x_copy(p).start())

    @pl.when(polar)
    def _():
        for copy in copies:
            copy.start()

    spacing = math.pi / (rows * count)
    place = (device * rows + row).astype(jnp.float32)
    center = jnp.sin((place + 0.5) * spacing)
    ratio_s[0] = jnp.sin((place + 1.0) * spacing) / center
    ratio_s[1] = jnp.sin(place * spacing) / center

    def prepare(level, carry):
        for t in range(tiles):
            chn_s[level, :, LANES * t : LANES * (t + 1)] = second(tile_of(cn_ref, level, t))
        return carry

    lax.fori_loop(0, levels, prepare, 0)

    def increments(p, level, put):
        rn, rs = ratio_s[0], ratio_s[1]

        def edge(k, t, target):
            at = pl.ds(pl.multiple_of(p // 8 * 8, 8), 8)
            if t < full:
                value = edge_ref[k, at, LANES * t : LANES * (t + 1)]
            else:
                value = jnp.concatenate(
                    [edge_ref[k, at, LANES * full : width], edge_ref[k, at, : LANES - rest]], axis=1
                )
            value = pltpu.roll(value, lax.rem(target + 8 - lax.rem(p, 8), 8), 0)
            return jnp.concatenate([value] * (rows // 8), axis=0)

        for t in range(tiles):
            inc_x = tile_of(x_ref, p, t)
            here = tile_of(q_ref, p, t)
            cn = tile_of(cn_ref, level, t)
            chn = chn_s[level, :, LANES * t : LANES * (t + 1)]
            q_north = jnp.where(row == rows - 1, edge(1, t, 7), pltpu.roll(here, rows - 1, 0))
            dy = q_north - here
            dy_south = jnp.where(row == 0, here - edge(3, t, 0), pltpu.roll(dy, 1, 0))
            sy = min_mod(dy, dy_south)
            sy_north = jnp.where(row == rows - 1, edge(2, t, 7), pltpu.roll(sy, rows - 1, 0))
            north = upwind(cn, chn, here, sy, q_north, sy_north)
            south = jnp.where(row == 0, edge(0, t, 0), pltpu.roll(north, 1, 0))
            put(t, here, inc_x + (rs * south - rn * north))

    def respond():
        half = width // 2
        filters = spectrum_ref.shape[0]
        spot = lax.broadcasted_iota(jnp.int32, (rows, filters), 0)
        picked = jnp.zeros((rows, filters), jnp.int32)
        for j in range(rows):
            picked = jnp.where(spot == j, index_ref[device * rows + j], picked)
        one_hot = picked == lax.broadcasted_iota(jnp.int32, (rows, filters), 1)
        one_hot = one_hot.astype(jnp.float32).astype(jnp.bfloat16)
        for start in range(0, width, 2 * CHUNK):
            span = slice(start, min(start + 2 * CHUNK, width))
            value = spectrum_ref[:, span]
            chosen = jnp.zeros((rows, span.stop - start), jnp.float32)
            for _ in range(3):
                piece = value.astype(jnp.bfloat16)
                chosen = chosen + jnp.dot(one_hot, piece, preferred_element_type=jnp.float32)
                value = value - piece.astype(jnp.float32)
            chosen_s[:, span] = chosen
        blocks = 4 * deep // CHUNK
        chosen_s[:, width:] = jnp.zeros((rows, CHUNK * blocks - width), jnp.float32)
        column = lax.broadcasted_iota(jnp.int32, (rows, CHUNK), 1)
        parts = []
        for b in range(blocks):
            here = column + CHUNK * b
            weight = jnp.where((here == 0) | (here == half), 1.0 / width, 2.0 / width)
            value = chosen_s[:, CHUNK * b : CHUNK * (b + 1)] * weight
            for _ in range(3):
                piece = value.astype(jnp.bfloat16)
                parts.append(piece)
                value = value - piece.astype(jnp.float32)
        moved = jnp.dot(jnp.concatenate(parts, axis=0), order_ref[...], preferred_element_type=jnp.float32)
        moved = moved.reshape(blocks, 3, rows, CHUNK)
        moved = moved[:, 0] + moved[:, 1] + moved[:, 2]
        low_half = lane < LANES // 2
        for b in range(blocks):
            at = 2 * deep + LANES * b
            resp_ref[:, at : at + LANES] = moved[b, :, LANES:]
        for b in range(0, blocks, 2):
            at = LANES // 2 * b
            a, c = moved[b, :, :LANES], moved[b + 1, :, :LANES]
            resp_ref[:, at : at + LANES] = jnp.where(low_half, a, pltpu.roll(c, LANES // 2, 1))
            resp_ref[:, deep + at : deep + at + LANES] = jnp.where(
                low_half, pltpu.roll(a, LANES // 2, 1), c
            )

    @pl.when(jnp.logical_not(polar))
    def _():
        def plane(p, carry):
            def put(t, here, inc):
                size = LANES if t < full else rest
                out_ref[p, :, LANES * t : LANES * t + size] = (here + inc)[:, :size]

            q_copy(p).wait()
            x_copy(p).wait()
            increments(p, lax.rem(p, levels), put)
            out_copy(p).start()
            return carry

        lax.fori_loop(0, planes, plane, 0)

    @pl.when(polar)
    def _():
        def plane(p, carry):
            def put(t, here, inc):
                if t >= full:
                    inc = jnp.where(lane < rest, inc, 0.0)
                inc_s[:, LANES * t : LANES * (t + 1)] = inc

            q_copy(p).wait()
            x_copy(p).wait()
            increments(p, lax.rem(p, levels), put)
            x0, x1, x2, x3 = (inc_s[:, part * k : part * k + deep] for k in range(4))
            a, b = x0 + x2, x1 + x3
            where = pl.ds(pl.multiple_of(p * rows, rows), rows)
            for k, y in enumerate((a + b, a - b, x0 - x2, x1 - x3)):
                y_s[where, deep * k : deep * (k + 1)] = y.astype(jnp.bfloat16)
            return carry

        lax.fori_loop(0, planes, plane, 0)
        total = planes * rows
        respond()

        def forward(y, matrix, at):
            coefficients = jnp.dot(y, matrix, preferred_element_type=jnp.float32)
            scaled = coefficients.reshape(planes, rows, CHUNK) * resp_ref[:, at : at + CHUNK][None]
            s_s[:, at : at + CHUNK] = scaled.reshape(total, CHUNK).astype(jnp.bfloat16)

        copies[0].wait()
        for k in range(2):
            for n in range(deep // CHUNK):
                forward(
                    y_s[:, deep * k : deep * (k + 1)],
                    even_s[k, :, CHUNK * n : CHUNK * (n + 1)],
                    deep * k + CHUNK * n,
                )
        copies[1].wait()
        for n in range(2 * deep // CHUNK):
            forward(
                y_s[:, 2 * deep :], odd_s[:, CHUNK * n : CHUNK * (n + 1)], 2 * deep + CHUNK * n
            )
        copies[2].wait()
        copies[3].wait()
        for n in range(deep // CHUNK):
            span = slice(CHUNK * n, CHUNK * (n + 1))
            size = min(CHUNK, part - CHUNK * n)

            def back(scaled, matrix):
                return jnp.dot(scaled, matrix, preferred_element_type=jnp.float32)

            e0 = back(s_s[:, :deep], even_t_s[0, :, span])
            e2 = back(s_s[:, deep : 2 * deep], even_t_s[1, :, span])
            eu = back(s_s[:, 2 * deep :], odd_t_s[:, span])
            ev = back(s_s[:, 2 * deep :], odd_t_s[:, deep + CHUNK * n : deep + CHUNK * (n + 1)])
            plus, minus = e0 + e2, e0 - e2
            for k, value in enumerate((plus + eu, minus + ev, plus - eu, minus - ev)):
                start = part * k + CHUNK * n
                out_ref[:, :, start : start + size] = (
                    q_ref[:, :, start : start + size]
                    + value.reshape(planes, rows, CHUNK)[:, :, :size]
                )
        over_planes(lambda p: out_copy(p).start())

    over_planes(lambda p: out_copy(p).wait())


def on_device(tracers, east_courant, north_courant, spectrum, filter_index):
    fields, levels, rows, width = tracers.shape
    planes = fields * levels
    devices = lax.axis_size("lon")
    device = lax.axis_index("lon")
    part = width // 4
    deep = up_to(part, CHUNK)
    wide = up_to(width, LANES)
    stacked = up_to(planes + levels, 8)
    q = tracers.reshape(planes, rows, width)
    kind = jnp.bfloat16
    vmem = pl.BlockSpec(memory_space=pltpu.VMEM)
    smem = pl.BlockSpec(memory_space=pltpu.SMEM)
    anywhere = pl.BlockSpec(memory_space=pl.ANY)
    edge, along = pl.pallas_call(
        functools.partial(exchange, devices),
        out_shape=(
            jax.ShapeDtypeStruct((4, stacked, width), jnp.float32),
            jax.ShapeDtypeStruct(q.shape, jnp.float32),
        ),
        in_specs=[anywhere] * 3,
        out_specs=(vmem, anywhere),
        scratch_shapes=[
            pltpu.VMEM((planes, 8, width), jnp.float32),
            pltpu.VMEM((planes, 8, width), jnp.float32),
            pltpu.VMEM((levels, 8, width), jnp.float32),
            pltpu.VMEM((levels, rows, width), jnp.float32),
            pltpu.VMEM((levels, rows, wide), jnp.float32),
            pltpu.VMEM((planes, rows, width), jnp.float32),
            pltpu.VMEM((2, 2 * stacked, width), jnp.float32),
        ]
        + [pltpu.VMEM((2 * stacked, width), kind)] * 4
        + [pltpu.SemaphoreType.DMA((n,)) for n in (4, 2, 2, planes)],
        compiler_params=pltpu.CompilerParams(
            collective_id=0, has_side_effects=True, vmem_limit_bytes=56 * 2**20
        ),
    )(q, east_courant, north_courant)
    matrices = [jnp.asarray(m) for m in make_matrices(width)]
    out = pl.pallas_call(
        functools.partial(kernel, width, devices),
        out_shape=jax.ShapeDtypeStruct(q.shape, jnp.float32),
        in_specs=[smem, smem, anywhere] + [anywhere] + [vmem] * 4 + [anywhere] * 4,
        out_specs=anywhere,
        scratch_shapes=[
            pltpu.VMEM((planes, rows, width), jnp.float32),
            pltpu.VMEM((planes, rows, width), jnp.float32),
            pltpu.VMEM((planes, rows, width), jnp.float32),
            pltpu.VMEM((rows, 4 * deep), jnp.float32),
            pltpu.VMEM((rows, 4 * deep), jnp.float32),
            pltpu.VMEM((2, rows, LANES), jnp.float32),
            pltpu.VMEM((levels, rows, wide), jnp.float32),
            pltpu.VMEM((rows, 3 * part + deep + LANES), jnp.float32),
            pltpu.VMEM((planes * rows, 4 * deep), kind),
            pltpu.VMEM((planes * rows, 4 * deep), kind),
        ]
        + [pltpu.VMEM(m.shape, kind) for m in matrices]
        + [pltpu.SemaphoreType.DMA((n,)) for n in (4, planes, planes, planes)],
        compiler_params=pltpu.CompilerParams(vmem_limit_bytes=56 * 2**20),
    )(
        device.astype(jnp.int32).reshape(1), filter_index, q, along, north_courant, edge,
        spectrum, jnp.asarray(make_order()), *matrices,
    )
    return out.reshape(tracers.shape)


def solution(mesh):
    placed = (P("grp", None, "lon", None), P("grp", "lon", None), P("grp", "lon", None), P(), P())
    return jax.shard_map(
        on_device,
        mesh=mesh,
        in_specs=placed,
        out_specs=P("grp", None, "lon", None),
        check_vma=False,
    )
```

```python
import functools
import math

import jax
import jax.numpy as jnp
import ml_dtypes
import numpy as np
from jax import lax
from jax.experimental import pallas as pl
from jax.experimental.pallas import tpu as pltpu
from jax.sharding import PartitionSpec as P

LANES = 128
CHUNK = 256


def up_to(value, multiple):
    return -(-value // multiple) * multiple


def column_groups(width):
    half = width // 2
    column = np.arange(width)
    number = np.where(column <= half, column, column - half)
    return number, [np.where(number % 4 == 0)[0], np.where(number % 4 == 2)[0], np.where(number % 2 == 1)[0]]


def make_matrices(width):
    half, part = width // 2, width // 4
    deep = up_to(part, CHUNK)
    number, groups = column_groups(width)
    points = np.arange(half, dtype=np.int64)[:, None]
    angle = ((points * number[None, :]) % width) * (2.0 * math.pi / width)
    basis = np.where(np.arange(width)[None, :] <= half, np.cos(angle), np.sin(angle))
    even = np.zeros((2, deep, deep), np.float64)
    for at in range(2):
        even[at, :part, : len(groups[at])] = basis[:part, groups[at]]
    odd = np.zeros((2, deep, 2 * deep), np.float64)
    odd[0, :part, : len(groups[2])] = basis[:part, groups[2]]
    odd[1, :part, : len(groups[2])] = basis[part:, groups[2]]
    odd = odd.reshape(2 * deep, 2 * deep)
    kind = ml_dtypes.bfloat16
    return (
        even.astype(kind),
        odd.astype(kind),
        np.ascontiguousarray(even.transpose(0, 2, 1)).astype(kind),
        np.ascontiguousarray(odd.T).astype(kind),
    )


def make_order():
    at = np.arange(CHUNK)
    source = np.concatenate([at[at % 4 == 0], at[at % 4 == 2], at[at % 2 == 1]])
    order = np.zeros((CHUNK, CHUNK), np.float32)
    order[source, at] = 1.0
    return order.astype(ml_dtypes.bfloat16)


def tile_of(ref, at, t):
    width = ref.shape[-1]
    if LANES * (t + 1) <= width:
        return ref[at, :, LANES * t : LANES * (t + 1)]
    start = LANES * t
    return jnp.concatenate([ref[at, :, start:width], ref[at, :, : start + LANES - width]], axis=1)


def east_west(width, rows, load_q, load_c, load_ch, put):
    tiles = -(-width // LANES)
    rest = width % LANES
    lane = lax.broadcasted_iota(jnp.int32, (rows, LANES), 1)
    memo = {}

    def cached(function):
        def call(t):
            key = (function.__name__, t)
            if key not in memo:
                memo[key] = function(t)
            return memo[key]

        return call

    def wrapped(load, t):
        if t >= 0:
            return load(min(t, tiles - 1))
        return pltpu.roll(load(tiles - 1), LANES - rest, 1) if rest else load(tiles - 1)

    @cached
    def q(t):
        return wrapped(load_q, t)

    @cached
    def q_left(t):
        return pltpu.roll(q(t), LANES - 1, 1)

    @cached
    def q_east(t):
        return jnp.where(lane == LANES - 1, q_left(min(t + 1, tiles - 1)), q_left(t))

    @cached
    def d(t):
        return q_east(t) - q(t)

    @cached
    def d_right(t):
        return pltpu.roll(d(t), 1, 1)

    @cached
    def s(t):
        return min_mod(d(t), jnp.where(lane == 0, d_right(max(t - 1, -1)), d_right(t)))

    @cached
    def s_left(t):
        return pltpu.roll(s(t), LANES - 1, 1)

    @cached
    def east(t):
        s_east = jnp.where(lane == LANES - 1, s_left(min(t + 1, tiles - 1)), s_left(t))
        c = wrapped(load_c, t)
        ch = wrapped(load_ch, t)
        return upwind(c, ch, q(t), s(t), q_east(t), s_east)

    @cached
    def east_right(t):
        return pltpu.roll(east(t), 1, 1)

    for t in range(tiles):
        put(t, jnp.where(lane == 0, east_right(t - 1), east_right(t)) - east(t))


def exchange(count, q_hbm, ce_hbm, cn_hbm, edge_ref, x_hbm, south_s, north_s, cn_s, ce_s, che_s, x_s, packs, up_s, down_s, low_s, high_s,
             local, send, recv, x_sems):
    planes, rows, width = q_hbm.shape
    levels = cn_hbm.shape[0]
    deep = edge_ref.shape[1]
    me = lax.axis_index("lon")
    last = count - 1
    loads = [
        pltpu.make_async_copy(q_hbm.at[:, pl.ds(rows - 8, 8), :], north_s, local.at[0]),
        pltpu.make_async_copy(cn_hbm.at[:, pl.ds(rows - 8, 8), :], cn_s, local.at[1]),
        pltpu.make_async_copy(q_hbm.at[:, pl.ds(0, 8), :], south_s, local.at[2]),
        pltpu.make_async_copy(ce_hbm, ce_s, local.at[3]),
    ]
    for load in loads:
        load.start()
    barrier = pltpu.get_barrier_semaphore()

    @pl.when(me > 0)
    def _():
        pl.semaphore_signal(barrier, inc=1, device_id={"lon": me - 1}, device_id_type=pl.DeviceIdType.MESH)

    @pl.when(me < last)
    def _():
        pl.semaphore_signal(barrier, inc=1, device_id={"lon": me + 1}, device_id_type=pl.DeviceIdType.MESH)

    for at in range(2):
        packs[at, 2 * deep - levels :, :] = jnp.zeros((levels, width), jnp.float32)
        packs[at, planes:deep, :] = jnp.zeros((levels, width), jnp.float32)

    loads[0].wait()
    loads[1].wait()
    for p in range(planes):
        packs[0, p : p + 1, :] = north_s[p, 6:7, :]
        packs[0, deep + p : deep + p + 1, :] = north_s[p, 7:8, :]
    for p in range(levels):
        packs[0, planes + p : planes + p + 1, :] = cn_s[p, 7:8, :]
    up_s[...] = packs[0].astype(jnp.bfloat16)

    outer = jnp.logical_or(me == 0, me == last)

    @pl.when(outer)
    def _():
        pl.semaphore_wait(barrier, 1)

    @pl.when(jnp.logical_not(outer))
    def _():
        pl.semaphore_wait(barrier, 2)

    up = pltpu.make_async_remote_copy(
        src_ref=up_s, dst_ref=low_s, send_sem=send.at[0], recv_sem=recv.at[0],
        device_id={"lon": me + 1}, device_id_type=pl.DeviceIdType.MESH,
    )
    down = pltpu.make_async_remote_copy(
        src_ref=down_s, dst_ref=high_s, send_sem=send.at[1], recv_sem=recv.at[1],
        device_id={"lon": me - 1}, device_id_type=pl.DeviceIdType.MESH,
    )

    @pl.when(me < last)
    def _():
        up.start()

    loads[2].wait()
    for p in range(planes):
        packs[1, p : p + 1, :] = south_s[p, 0:1, :]
        packs[1, deep + p : deep + p + 1, :] = south_s[p, 1:2, :]
    down_s[...] = packs[1].astype(jnp.bfloat16)

    @pl.when(me > 0)
    def _():
        down.start()

    loads[3].wait()
    tiles = -(-width // LANES)

    def prepare(level, carry):
        for t in range(tiles):
            che_s[level, :, LANES * t : LANES * (t + 1)] = second(tile_of(ce_s, level, t))
        return carry

    lax.fori_loop(0, levels, prepare, 0)

    def x_copy(p):
        return pltpu.make_async_copy(x_s.at[p], x_hbm.at[p], x_sems.at[p])

    def plane(p, level):
        def put(t, value):
            size = min(LANES, width - LANES * t)
            x_s[p, :, LANES * t : LANES * t + size] = value[:, :size]

        def load_q(t):
            return jnp.concatenate([tile_of(south_s, p, t), tile_of(north_s, p, t)], axis=0)

        east_west(
            width, rows, load_q, lambda t: tile_of(ce_s, level, t),
            lambda t: che_s[level, :, LANES * t : LANES * (t + 1)], put,
        )

    def together(level, carry):
        group = [field * levels + level for field in range(planes // levels)]
        for p in group:
            plane(p, level)
        for p in group:
            x_copy(p).start()
        return carry

    lax.fori_loop(0, levels, together, 0)

    @pl.when(me > 0)
    def _():
        up.wait_recv()

    @pl.when(me == 0)
    def _():
        low_s[...] = jnp.zeros_like(low_s)

    @pl.when(me < last)
    def _():
        down.wait_recv()

    @pl.when(me == last)
    def _():
        high_s[...] = jnp.zeros_like(high_s)

    for start in range(0, width, LANES):
        span = slice(start, min(start + LANES, width))
        low = low_s[:, span].astype(jnp.float32)
        high = high_s[:, span].astype(jnp.float32)
        low0, low1, high0, high1 = low[:deep], low[deep:], high[:deep], high[deep:]
        q0, q1, q_last = packs[1, :deep, span], packs[1, deep:, span], packs[0, deep:, span]
        cs = jnp.concatenate([low[planes : planes + levels]] * (deep // levels), axis=0)
        dy = q0 - low1
        edge_ref[0, :, span] = upwind(
            cs, second(cs), low1, min_mod(dy, low1 - low0), q0, min_mod(q1 - q0, dy)
        )
        edge_ref[1, :, span] = high0
        edge_ref[2, :, span] = min_mod(high1 - high0, high0 - q_last)
        edge_ref[3, :, span] = low1

    @pl.when(me < last)
    def _():
        up.wait_send()

    @pl.when(me > 0)
    def _():
        down.wait_send()

    def finish(p, carry):
        x_copy(p).wait()
        return carry

    lax.fori_loop(0, planes, finish, 0)


def min_mod(a, b):
    return jnp.maximum(jnp.minimum(a, jnp.maximum(b, 0.0)), jnp.minimum(b, 0.0))


def upwind(c, ch, ql, sl, qr, sr):
    ahead = c > 0.0
    return c * jnp.where(ahead, ql, qr) + ch * jnp.where(ahead, sl, sr)


def second(c):
    return c * (jnp.where(c > 0.0, 0.5, -0.5) - 0.5 * c)


def kernel(width, count, where_ref, index_ref, q_hbm, x_hbm, cn_ref, edge_ref, spectrum_ref, order_ref,
           even_hbm, odd_hbm, even_t_hbm, odd_t_hbm, out_hbm,
           q_ref, x_ref, out_ref, chosen_s, resp_ref, ratio_s, chn_s, inc_s, y_s, s_s,
           even_s, odd_s, even_t_s, odd_t_s, sems, in_sems, x_sems, out_sems):
    planes, rows, _ = q_ref.shape
    levels = cn_ref.shape[0]
    part = width // 4
    deep = up_to(part, CHUNK)
    full = width // LANES
    rest = width - full * LANES
    tiles = full + (1 if rest else 0)
    lane = lax.broadcasted_iota(jnp.int32, (rows, LANES), 1)
    row = lax.broadcasted_iota(jnp.int32, (rows, LANES), 0)
    copies = [
        pltpu.make_async_copy(source, target, sems.at[at])
        for at, (source, target) in enumerate(
            ((even_hbm, even_s), (odd_hbm, odd_s), (even_t_hbm, even_t_s), (odd_t_hbm, odd_t_s))
        )
    ]
    device = where_ref[0]
    quarter = count // 4
    polar = jnp.logical_or(device < quarter, device >= count - quarter)

    def q_copy(p):
        return pltpu.make_async_copy(q_hbm.at[p], q_ref.at[p], in_sems.at[p])

    def x_copy(p):
        return pltpu.make_async_copy(x_hbm.at[p], x_ref.at[p], x_sems.at[p])

    def out_copy(p):
        return pltpu.make_async_copy(out_ref.at[p], out_hbm.at[p], out_sems.at[p])

    def over_planes(act):
        lax.fori_loop(0, planes, lambda p, carry: (act(p), carry)[1], 0)

    def begin(level, carry):
        for field in range(planes // levels):
            q_copy(field * levels + level).start()
            x_copy(field * levels + level).start()
        return carry

    lax.fori_loop(0, levels, begin, 0)

    @pl.when(polar)
    def _():
        for copy in copies:
            copy.start()

    spacing = math.pi / (rows * count)
    place = (device * rows + row).astype(jnp.float32)
    center = jnp.sin((place + 0.5) * spacing)
    ratio_s[0] = jnp.sin((place + 1.0) * spacing) / center
    ratio_s[1] = jnp.sin(place * spacing) / center

    def prepare(level, carry):
        for t in range(tiles):
            chn_s[level, :, LANES * t : LANES * (t + 1)] = second(tile_of(cn_ref, level, t))
        return carry

    lax.fori_loop(0, levels, prepare, 0)

    def increments(p, level, put):
        rn, rs = ratio_s[0], ratio_s[1]

        def edge(k, t, target):
            at = pl.ds(pl.multiple_of(p // 8 * 8, 8), 8)
            if t < full:
                value = edge_ref[k, at, LANES * t : LANES * (t + 1)]
            else:
                value = jnp.concatenate(
                    [edge_ref[k, at, LANES * full : width], edge_ref[k, at, : LANES - rest]], axis=1
                )
            value = pltpu.roll(value, lax.rem(target + 8 - lax.rem(p, 8), 8), 0)
            return jnp.concatenate([value] * (rows // 8), axis=0)

        for t in range(tiles):
            inc_x = tile_of(x_ref, p, t)
            here = tile_of(q_ref, p, t)
            cn = tile_of(cn_ref, level, t)
            chn = chn_s[level, :, LANES * t : LANES * (t + 1)]
            q_north = jnp.where(row == rows - 1, edge(1, t, 7), pltpu.roll(here, rows - 1, 0))
            dy = q_north - here
            dy_south = jnp.where(row == 0, here - edge(3, t, 0), pltpu.roll(dy, 1, 0))
            sy = min_mod(dy, dy_south)
            sy_north = jnp.where(row == rows - 1, edge(2, t, 7), pltpu.roll(sy, rows - 1, 0))
            north = upwind(cn, chn, here, sy, q_north, sy_north)
            south = jnp.where(row == 0, edge(0, t, 0), pltpu.roll(north, 1, 0))
            put(t, here, inc_x + (rs * south - rn * north))

    def respond():
        half = width // 2
        filters = spectrum_ref.shape[0]
        spot = lax.broadcasted_iota(jnp.int32, (rows, filters), 0)
        picked = jnp.zeros((rows, filters), jnp.int32)
        for j in range(rows):
            picked = jnp.where(spot == j, index_ref[device * rows + j], picked)
        one_hot = picked == lax.broadcasted_iota(jnp.int32, (rows, filters), 1)
        one_hot = one_hot.astype(jnp.float32).astype(jnp.bfloat16)
        for start in range(0, width, 2 * CHUNK):
            span = slice(start, min(start + 2 * CHUNK, width))
            value = spectrum_ref[:, span]
            chosen = jnp.zeros((rows, span.stop - start), jnp.float32)
            for _ in range(3):
                piece = value.astype(jnp.bfloat16)
                chosen = chosen + jnp.dot(one_hot, piece, preferred_element_type=jnp.float32)
                value = value - piece.astype(jnp.float32)
            chosen_s[:, span] = chosen
        blocks = 4 * deep // CHUNK
        chosen_s[:, width:] = jnp.zeros((rows, CHUNK * blocks - width), jnp.float32)
        column = lax.broadcasted_iota(jnp.int32, (rows, CHUNK), 1)
        parts = []
        for b in range(blocks):
            here = column + CHUNK * b
            weight = jnp.where((here == 0) | (here == half), 1.0 / width, 2.0 / width)
            value = chosen_s[:, CHUNK * b : CHUNK * (b + 1)] * weight
            for _ in range(3):
                piece = value.astype(jnp.bfloat16)
                parts.append(piece)
                value = value - piece.astype(jnp.float32)
        moved = jnp.dot(jnp.concatenate(parts, axis=0), order_ref[...], preferred_element_type=jnp.float32)
        moved = moved.reshape(blocks, 3, rows, CHUNK)
        moved = moved[:, 0] + moved[:, 1] + moved[:, 2]
        low_half = lane < LANES // 2
        for b in range(blocks):
            at = 2 * deep + LANES * b
            resp_ref[:, at : at + LANES] = moved[b, :, LANES:]
        for b in range(0, blocks, 2):
            at = LANES // 2 * b
            a, c = moved[b, :, :LANES], moved[b + 1, :, :LANES]
            resp_ref[:, at : at + LANES] = jnp.where(low_half, a, pltpu.roll(c, LANES // 2, 1))
            resp_ref[:, deep + at : deep + at + LANES] = jnp.where(
                low_half, pltpu.roll(a, LANES // 2, 1), c
            )

    @pl.when(jnp.logical_not(polar))
    def _():
        def plane(p, level):
            def put(t, here, inc):
                size = LANES if t < full else rest
                out_ref[p, :, LANES * t : LANES * t + size] = (here + inc)[:, :size]

            increments(p, level, put)

        def together(level, carry):
            group = [field * levels + level for field in range(planes // levels)]
            for p in group:
                q_copy(p).wait()
                x_copy(p).wait()
            for p in group:
                plane(p, level)
            for p in group:
                out_copy(p).start()
            return carry

        lax.fori_loop(0, levels, together, 0)

    @pl.when(polar)
    def _():
        def plane(p, level, slot):
            def put(t, here, inc):
                if t >= full:
                    inc = jnp.where(lane < rest, inc, 0.0)
                inc_s[slot, :, LANES * t : LANES * (t + 1)] = inc

            increments(p, level, put)
            x0, x1, x2, x3 = (inc_s[slot, :, part * k : part * k + deep] for k in range(4))
            a, b = x0 + x2, x1 + x3
            where = pl.ds(pl.multiple_of(p * rows, rows), rows)
            for k, y in enumerate((a + b, a - b, x0 - x2, x1 - x3)):
                y_s[where, deep * k : deep * (k + 1)] = y.astype(jnp.bfloat16)

        def together(level, carry):
            group = [field * levels + level for field in range(planes // levels)]
            for p in group:
                q_copy(p).wait()
                x_copy(p).wait()
            for slot, p in enumerate(group):
                plane(p, level, slot)
            return carry

        lax.fori_loop(0, levels, together, 0)
        total = planes * rows
        respond()

        def forward(y, matrix, at):
            coefficients = jnp.dot(y, matrix, preferred_element_type=jnp.float32)
            scaled = coefficients.reshape(planes, rows, CHUNK) * resp_ref[:, at : at + CHUNK][None]
            s_s[:, at : at + CHUNK] = scaled.reshape(total, CHUNK).astype(jnp.bfloat16)

        copies[0].wait()
        for k in range(2):
            for n in range(deep // CHUNK):
                forward(
                    y_s[:, deep * k : deep * (k + 1)],
                    even_s[k, :, CHUNK * n : CHUNK * (n + 1)],
                    deep * k + CHUNK * n,
                )
        copies[1].wait()
        for n in range(2 * deep // CHUNK):
            forward(
                y_s[:, 2 * deep :], odd_s[:, CHUNK * n : CHUNK * (n + 1)], 2 * deep + CHUNK * n
            )
        copies[2].wait()
        copies[3].wait()
        for n in range(deep // CHUNK):
            span = slice(CHUNK * n, CHUNK * (n + 1))
            size = min(CHUNK, part - CHUNK * n)

            def back(scaled, matrix):
                return jnp.dot(scaled, matrix, preferred_element_type=jnp.float32)

            e0 = back(s_s[:, :deep], even_t_s[0, :, span])
            e2 = back(s_s[:, deep : 2 * deep], even_t_s[1, :, span])
            eu = back(s_s[:, 2 * deep :], odd_t_s[:, span])
            ev = back(s_s[:, 2 * deep :], odd_t_s[:, deep + CHUNK * n : deep + CHUNK * (n + 1)])
            plus, minus = e0 + e2, e0 - e2
            for k, value in enumerate((plus + eu, minus + ev, plus - eu, minus - ev)):
                start = part * k + CHUNK * n
                out_ref[:, :, start : start + size] = (
                    q_ref[:, :, start : start + size]
                    + value.reshape(planes, rows, CHUNK)[:, :, :size]
                )
        over_planes(lambda p: out_copy(p).start())

    over_planes(lambda p: out_copy(p).wait())


def on_device(tracers, east_courant, north_courant, spectrum, filter_index):
    fields, levels, rows, width = tracers.shape
    planes = fields * levels
    devices = lax.axis_size("lon")
    device = lax.axis_index("lon")
    part = width // 4
    deep = up_to(part, CHUNK)
    wide = up_to(width, LANES)
    stacked = up_to(planes + levels, 8)
    q = tracers.reshape(planes, rows, width)
    kind = jnp.bfloat16
    vmem = pl.BlockSpec(memory_space=pltpu.VMEM)
    smem = pl.BlockSpec(memory_space=pltpu.SMEM)
    anywhere = pl.BlockSpec(memory_space=pl.ANY)
    edge, along = pl.pallas_call(
        functools.partial(exchange, devices),
        out_shape=(
            jax.ShapeDtypeStruct((4, stacked, width), jnp.float32),
            jax.ShapeDtypeStruct(q.shape, jnp.float32),
        ),
        in_specs=[anywhere] * 3,
        out_specs=(vmem, anywhere),
        scratch_shapes=[
            pltpu.VMEM((planes, 8, width), jnp.float32),
            pltpu.VMEM((planes, 8, width), jnp.float32),
            pltpu.VMEM((levels, 8, width), jnp.float32),
            pltpu.VMEM((levels, rows, width), jnp.float32),
            pltpu.VMEM((levels, rows, wide), jnp.float32),
            pltpu.VMEM((planes, rows, width), jnp.float32),
            pltpu.VMEM((2, 2 * stacked, width), jnp.float32),
        ]
        + [pltpu.VMEM((2 * stacked, width), kind)] * 4
        + [pltpu.SemaphoreType.DMA((n,)) for n in (4, 2, 2, planes)],
        compiler_params=pltpu.CompilerParams(
            collective_id=0, has_side_effects=True, vmem_limit_bytes=56 * 2**20
        ),
    )(q, east_courant, north_courant)
    matrices = [jnp.asarray(m) for m in make_matrices(width)]
    out = pl.pallas_call(
        functools.partial(kernel, width, devices),
        out_shape=jax.ShapeDtypeStruct(q.shape, jnp.float32),
        in_specs=[smem, smem, anywhere] + [anywhere] + [vmem] * 4 + [anywhere] * 4,
        out_specs=anywhere,
        scratch_shapes=[
            pltpu.VMEM((planes, rows, width), jnp.float32),
            pltpu.VMEM((planes, rows, width), jnp.float32),
            pltpu.VMEM((planes, rows, width), jnp.float32),
            pltpu.VMEM((rows, 4 * deep), jnp.float32),
            pltpu.VMEM((rows, 4 * deep), jnp.float32),
            pltpu.VMEM((2, rows, LANES), jnp.float32),
            pltpu.VMEM((levels, rows, wide), jnp.float32),
            pltpu.VMEM((fields, rows, 3 * part + deep + LANES), jnp.float32),
            pltpu.VMEM((planes * rows, 4 * deep), kind),
            pltpu.VMEM((planes * rows, 4 * deep), kind),
        ]
        + [pltpu.VMEM(m.shape, kind) for m in matrices]
        + [pltpu.SemaphoreType.DMA((n,)) for n in (4, planes, planes, planes)],
        compiler_params=pltpu.CompilerParams(vmem_limit_bytes=56 * 2**20),
    )(
        device.astype(jnp.int32).reshape(1), filter_index, q, along, north_courant, edge,
        spectrum, jnp.asarray(make_order()), *matrices,
    )
    return out.reshape(tracers.shape)


def solution(mesh):
    placed = (P("grp", None, "lon", None), P("grp", "lon", None), P("grp", "lon", None), P(), P())
    return jax.shard_map(
        on_device,
        mesh=mesh,
        in_specs=placed,
        out_specs=P("grp", None, "lon", None),
        check_vma=False,
    )
```
